256 devices in a mesh: strip: 32 (over z, y_lo, core), basis: 8 (over x, y_hi).
Axes of the slice: x: 4, y: 4 (y_hi: 2, y_lo: 2; y = y_hi * 2 + y_lo), z: 8, core: 2. Of those that a mesh axis runs over, the one named last changes fastest.
Arguments:
- sky_image: float32 [4096, 1024], P('strip', 'basis'), may hold values from -6 to 6
- dual_coeffs: float32 [8, 4096, 1024], P('basis', 'strip'), may hold values from -2 to 2
- thresholds: float32 [8, 4096, 1024], P('basis', 'strip'), may hold values from 0.05 to 1
Outputs:
- dual_next: float32 [8, 4096, 1024], P('basis', 'strip')
- adjoint_image: float32 [4096, 1024], P('strip', 'basis')
The draws below stay inside these ranges and needn't reach their ends.
All inputs are finite; a program needn't handle non-finite values.
Results may differ from the reference program's by a relative error of at most 0.00002.
Values sent between devices are 32-bit elements; how exact they have to be, the bound alone decides.
No kernel may reach another device: no remote copies, remote signals or barrier semaphores. Data moves between devices by JAX's collectives and lax.ppermute only.
A program may use at most 64 MiB of HBM per device.

```python
import math
import jax
import jax.numpy as jnp
import numpy as np

COLS = 1024
BASES = 8
LEVELS = 3
NX = 4096


def shard_levels(rng, extent, pieces, smallest, largest):
    loudness = 1.0
    for axis_at, parts in pieces:
        draws = jax.random.uniform(jax.random.fold_in(jax.random.fold_in(rng, 6), axis_at), (parts,), jnp.float32, smallest / len(pieces), largest / len(pieces))
        loudness = loudness * jnp.repeat(jnp.exp(draws), extent[axis_at] // parts).reshape((-1,) + (1,) * (len(extent) - 1 - axis_at))
    return loudness


def scatter_about(stream_key, shape, spread, reach, cuts=(), kind=jnp.bfloat16):
    loudness = shard_levels(stream_key, shape, cuts, -0.22, 0.18) if cuts else 1.0
    drawn = jax.random.normal(stream_key, shape, jnp.float32) * spread * loudness
    return jnp.minimum(jnp.maximum(drawn, -reach), reach).astype(kind)


def setup_inputs(seed: int = 0) -> dict:
    keys = jax.random.split(jax.random.key(seed), 4)
    return {
        "sky_image": scatter_about(keys[0], (NX, COLS), 1.0, 6.0, ((0, 32), (1, 8)), jnp.float32),
        "dual_coeffs": scatter_about(keys[1], (BASES, NX, COLS), 0.3, 2.0, ((0, 8), (1, 32)), jnp.float32),
        "thresholds": jnp.clip(jnp.exp(math.log(1.0) - 2.9957323 * jax.random.uniform(keys[2], (BASES, NX, COLS), jnp.float32) ** shard_levels(keys[2], (BASES, NX, COLS), ((0, 8), (1, 32)), -0.2, 0.2)), 0.05, 1.0),
    }


daubechies = [[0.7071067811865476, 0.7071067811865476], [0.48296291314469025, 0.836516303737469, 0.22414386804185735, -0.12940952255092145], [0.3326705529509569, 0.8068915093133388, 0.4598775021193313, -0.13501102001039084, -0.08544127388224149, 0.035226291882100656], [0.23037781330885523, 0.7148465705525415, 0.6308807679295904, -0.02798376941698385, -0.18703481171888114, 0.030841381835986965, 0.032883011666982945, -0.010597401784997278], [0.160102397974125, 0.6038292697974729, 0.7243085284385744, 0.13842814590110342, -0.24229488706619015, -0.03224486958502952, 0.07757149384006515, -0.006241490213011705, -0.012580751999015526, 0.003335725285001549], [0.11154074335008017, 0.4946238903983854, 0.7511339080215775, 0.3152503517092432, -0.22626469396516913, -0.12976686756709563, 0.09750160558707936, 0.02752286553001629, -0.031582039318031156, 0.0005538422009938016, 0.004777257511010651, -0.00107730108499558], [0.07785205408506236, 0.39653931948230575, 0.7291320908465551, 0.4697822874053586, -0.14390600392910627, -0.22403618499416572, 0.07130921926705004, 0.08061260915106681, -0.03802993693503463, -0.01657454163101562, 0.012550998556013784, 0.00042957797300470274, -0.0018016407039998328, 0.0003537138000010399], [0.05441584224308161, 0.3128715909144659, 0.6756307362980128, 0.5853546836548691, -0.015829105256023893, -0.2840155429624281, 0.00047248457399797254, 0.128747426620186, -0.01736930100202211, -0.04408825393106472, 0.013981027917015516, 0.008746094047015655, -0.00487035299301066, -0.0003917403729959771, 0.0006754494059985568, -0.00011747678400228192]]

def filter_table():
    low_rows = np.zeros((8, 16), np.float32)
    high_rows = np.zeros((8, 16), np.float32)
    for basis_row, filter_taps in enumerate(daubechies):
        length = len(filter_taps)
        for tap_index in range(length):
            low_rows[basis_row, tap_index] = filter_taps[tap_index]
            high_rows[basis_row, tap_index] = (-1) ** tap_index * filter_taps[length - 1 - tap_index]
    return (low_rows, high_rows)

def weave(first_part, second_part, band_axis):
    stacked = jnp.stack((first_part, second_part), axis=band_axis)
    if band_axis == -2:
        new_shape = first_part.shape[:-2] + (2 * first_part.shape[-2], first_part.shape[-1])
    else:
        new_shape = first_part.shape[:-1] + (2 * first_part.shape[-1],)
    return stacked.reshape(new_shape)

def phase_part(signal, offset, band_axis):
    if band_axis == -2:
        return signal[..., offset::2, :]
    return signal[..., offset::2]

def split_axis(signal, low_pass, high_pass, band_axis):
    even_part = phase_part(signal, 0, band_axis)
    odd_part = phase_part(signal, 1, band_axis)
    for tap_pair in range(8):
        even_roll = jnp.roll(even_part, -tap_pair, axis=band_axis)
        odd_roll = jnp.roll(odd_part, -tap_pair, axis=band_axis)
        low_term = low_pass[2 * tap_pair] * even_roll + low_pass[2 * tap_pair + 1] * odd_roll
        high_term = high_pass[2 * tap_pair] * even_roll + high_pass[2 * tap_pair + 1] * odd_roll
        if tap_pair == 0:
            low_band, high_band = (low_term, high_term)
        else:
            low_band, high_band = (low_band + low_term, high_band + high_term)
    return (low_band, high_band)

def merge_axis(low_band, high_band, low_pass, high_pass, band_axis):
    for tap_pair in range(8):
        low_roll = jnp.roll(low_band, tap_pair, axis=band_axis)
        high_roll = jnp.roll(high_band, tap_pair, axis=band_axis)
        even_term = low_pass[2 * tap_pair] * low_roll + high_pass[2 * tap_pair] * high_roll
        odd_term = low_pass[2 * tap_pair + 1] * low_roll + high_pass[2 * tap_pair + 1] * high_roll
        if tap_pair == 0:
            even_sum, odd_sum = (even_term, odd_term)
        else:
            even_sum, odd_sum = (even_sum + even_term, odd_sum + odd_term)
    return weave(even_sum, odd_sum, band_axis)

def analyse(signal, low_pass, high_pass, levels_left):
    top_half, bottom = split_axis(signal, low_pass, high_pass, -2)
    coarse, band_lh = split_axis(top_half, low_pass, high_pass, -1)
    band_hl, band_hh = split_axis(bottom, low_pass, high_pass, -1)
    if levels_left > 1:
        coarse = analyse(coarse, low_pass, high_pass, levels_left - 1)
    return weave(weave(coarse, band_lh, -1), weave(band_hl, band_hh, -1), -2)

def synthesize(coefficients, low_pass, high_pass, levels_left):
    coarse = coefficients[..., 0::2, 0::2]
    band_lh = coefficients[..., 0::2, 1::2]
    band_hl = coefficients[..., 1::2, 0::2]
    band_hh = coefficients[..., 1::2, 1::2]
    if levels_left > 1:
        coarse = synthesize(coarse, low_pass, high_pass, levels_left - 1)
    top_half = merge_axis(coarse, band_lh, low_pass, high_pass, -1)
    bottom = merge_axis(band_hl, band_hh, low_pass, high_pass, -1)
    return merge_axis(top_half, bottom, low_pass, high_pass, -2)

def reference(sky_image, dual_coeffs, thresholds):
    low_rows, high_rows = filter_table()
    norm_scale = 1.0 / math.sqrt(BASES)
    updated_list = []
    summed = jnp.zeros(sky_image.shape, jnp.float32)
    for basis_index in range(BASES):
        low_pass = [float(low_rows[basis_index, tap_index]) for tap_index in range(16)]
        high_pass = [float(high_rows[basis_index, tap_index]) for tap_index in range(16)]
        coefficients = analyse(sky_image, low_pass, high_pass, LEVELS) * norm_scale
        updated = jnp.clip(dual_coeffs[basis_index] + coefficients, -thresholds[basis_index], thresholds[basis_index])
        updated_list.append(updated)
        summed = summed + synthesize(updated, low_pass, high_pass, LEVELS)
    return (jnp.stack(updated_list), summed * norm_scale)
```

```python
import math

import jax
import jax.numpy as jnp
import numpy as np
from jax import lax
from jax.experimental import pallas as pl
from jax.experimental.pallas import tpu as pltpu
from jax.sharding import PartitionSpec as P

BASES = 8
ROWS = 128
COLS = 1024
TILE = 256
TAIL = 104
EXT = ROWS + TAIL
BANDS = 224


daubechies = [
    [0.7071067811865476, 0.7071067811865476],
    [0.48296291314469025, 0.836516303737469, 0.22414386804185735, -0.12940952255092145],
    [
        0.3326705529509569,
        0.8068915093133388,
        0.4598775021193313,
        -0.13501102001039084,
        -0.08544127388224149,
        0.035226291882100656,
    ],
    [
        0.23037781330885523,
        0.7148465705525415,
        0.6308807679295904,
        -0.02798376941698385,
        -0.18703481171888114,
        0.030841381835986965,
        0.032883011666982945,
        -0.010597401784997278,
    ],
    [
        0.160102397974125,
        0.6038292697974729,
        0.7243085284385744,
        0.13842814590110342,
        -0.24229488706619015,
        -0.03224486958502952,
        0.07757149384006515,
        -0.006241490213011705,
        -0.012580751999015526,
        0.003335725285001549,
    ],
    [
        0.11154074335008017,
        0.4946238903983854,
        0.7511339080215775,
        0.3152503517092432,
        -0.22626469396516913,
        -0.12976686756709563,
        0.09750160558707936,
        0.02752286553001629,
        -0.031582039318031156,
        0.0005538422009938016,
        0.004777257511010651,
        -0.00107730108499558,
    ],
    [
        0.07785205408506236,
        0.39653931948230575,
        0.7291320908465551,
        0.4697822874053586,
        -0.14390600392910627,
        -0.22403618499416572,
        0.07130921926705004,
        0.08061260915106681,
        -0.03802993693503463,
        -0.01657454163101562,
        0.012550998556013784,
        0.00042957797300470274,
        -0.0018016407039998328,
        0.0003537138000010399,
    ],
    [
        0.05441584224308161,
        0.3128715909144659,
        0.6756307362980128,
        0.5853546836548691,
        -0.015829105256023893,
        -0.2840155429624281,
        0.00047248457399797254,
        0.128747426620186,
        -0.01736930100202211,
        -0.04408825393106472,
        0.013981027917015516,
        0.008746094047015655,
        -0.00487035299301066,
        -0.0003917403729959771,
        0.0006754494059985568,
        -0.00011747678400228192,
    ],
]


def composed_filters():
    filters = []
    for taps in daubechies:
        length = len(taps)
        low = np.zeros(16)
        high = np.zeros(16)
        low[:length] = np.float32(taps)
        high[:length] = [(-1) ** k * np.float32(taps[length - 1 - k]) for k in range(length)]
        levels = [(low, high)]
        for level in (1, 2):
            coarse = levels[-1][0]
            step = 2**level
            size = len(coarse) + 15 * step
            pair = []
            for band in (low, high):
                longer = np.zeros(size)
                for k in range(16):
                    longer[k * step : k * step + len(coarse)] += band[k] * coarse
                pair.append(longer)
            levels.append(tuple(pair))
        filters.append(levels)
    return filters


def row_and_column_matrices():
    scale = 1.0 / math.sqrt(BASES)
    odd = list(range(1, ROWS, 2))
    two = list(range(2, ROWS, 4))
    four = list(range(0, ROWS, 4))
    order = [(1, r) for r in odd + two + four] + [(2, r) for r in two + four] + [(3, r) for r in four]
    rows = np.zeros((BASES, BANDS, EXT))
    columns = np.zeros((BASES, 3, TILE + 128, TILE))
    for basis, levels in enumerate(composed_filters()):
        for at, (level, row) in enumerate(order):
            half = 2 ** (level - 1)
            taps = levels[level - 1][(row // half) % 2]
            start = row - row % (2 * half)
            rows[basis, at, start : start + len(taps)] += taps * scale
        for level in (1, 2, 3):
            half = 2 ** (level - 1)
            for column in range(0, TILE, half):
                taps = levels[level - 1][(column // half) % 2]
                start = column - column % (2 * half)
                columns[basis, level - 1, start : start + len(taps), column] += taps
    return rows.astype(np.float32), columns.astype(np.float32)


def matmul(a, b):
    return lax.dot_general(
        a, b, (((1,), (0,)), ((), ())), precision=lax.Precision.HIGHEST, preferred_element_type=jnp.float32
    )


def matmul_t(a, b):
    return lax.dot_general(
        a, b, (((1,), (1,)), ((), ())), precision=lax.Precision.HIGHEST, preferred_element_type=jnp.float32
    )


def left_matmul_t(a, b):
    return lax.dot_general(
        a, b, (((0,), (0,)), ((), ())), precision=lax.Precision.HIGHEST, preferred_element_type=jnp.float32
    )


LEVEL_ROWS = ((0, 128), (128, 64), (192, 32))


def wavelet_kernel(basis_ref, image_ref, dual_ref, limit_ref, rows_ref, columns_ref, next_ref, adjoint_ref, bands, masked, woven):
    tiles = COLS // TILE
    row_op = rows_ref[0]
    for t in range(tiles):
        field = jnp.concatenate([image_ref[2 * t], image_ref[2 * t + 1]], axis=1)
        bands[:, t * TILE : (t + 1) * TILE] = matmul(row_op, field)
    column = lax.broadcasted_iota(jnp.int32, (32, TILE), 1)
    even = column % 2 == 0
    fourth = column % 4 == 0
    for t in range(tiles):
        at = slice(t * TILE, (t + 1) * TILE)
        ahead = (t + 1) % tiles * TILE
        out = []
        for level, (first, count) in enumerate(LEVEL_ROWS):
            main = matmul(bands[first : first + count, at], columns_ref[0, level, :TILE, :])
            rim = matmul(bands[first : first + count, ahead : ahead + 128], columns_ref[0, level, TILE:, 128:])
            out.append(jnp.concatenate([main[:, :128], main[:, 128:] + rim], axis=1))
        one, two, three = out
        coarse = (
            (1, 2, one[:64]),
            (2, 4, jnp.where(even, two[:32], one[64:96])),
            (0, 4, jnp.where(fourth, three, jnp.where(even, two[32:], one[96:]))),
        )
        halves = ((0, slice(0, 128)), (1, slice(128, TILE)))
        for first, stride, value in coarse:
            for h, lanes in halves:
                woven[2 * t + h, pl.ds(first, ROWS // stride, stride), :] = value[:, lanes]
        for h in range(2):
            here = slice((2 * t + h) * 128, (2 * t + h + 1) * 128)
            limit = limit_ref[0, :, here]
            fresh = jnp.minimum(jnp.maximum(dual_ref[0, :, here] + woven[2 * t + h], -limit), limit)
            next_ref[0, :, here] = fresh
            woven[2 * t + h] = fresh
        a, b, c = (
            jnp.concatenate([woven[2 * t + h, pl.ds(first, ROWS // stride, stride), :] for h in range(2)], axis=1)
            for first, stride, _ in coarse
        )
        masked[0:64, at] = a
        masked[64:96, at] = jnp.where(even, 0.0, b)
        masked[96:128, at] = jnp.where(even, 0.0, c)
        masked[128:160, at] = b
        masked[160:192, at] = jnp.where(fourth, 0.0, c)
        masked[192:224, at] = c
    for t in range(tiles):
        at = slice(t * TILE, (t + 1) * TILE)
        behind = (t + tiles - 1) % tiles * TILE + 128
        out = []
        for level, (first, count) in enumerate(LEVEL_ROWS):
            main = matmul_t(masked[first : first + count, at], columns_ref[0, level, :TILE, :])
            rim = matmul_t(masked[first : first + count, behind : behind + 128], columns_ref[0, level, TILE:, 128:])
            out.append(jnp.concatenate([main[:, :128] + rim, main[:, 128:]], axis=1))
        part = left_matmul_t(row_op, jnp.concatenate(out, axis=0))
        adjoint_ref[2 * t] = part[:, :128]
        adjoint_ref[2 * t + 1] = part[:, 128:]


def wavelet_update(basis, field, dual_coeffs, thresholds, row_ops, column_ops):
    whole = lambda shape: pl.BlockSpec(shape, lambda i, b: (0,) * len(shape))
    of_basis = lambda shape: pl.BlockSpec(shape, lambda i, b: (b[0],) + (0,) * (len(shape) - 1))
    grid_spec = pltpu.PrefetchScalarGridSpec(
        num_scalar_prefetch=1,
        grid=(1,),
        in_specs=[
            whole((8, EXT, 128)),
            whole((1, ROWS, COLS)),
            whole((1, ROWS, COLS)),
            of_basis((1, BANDS, EXT)),
            of_basis((1, 3, TILE + 128, TILE)),
        ],
        out_specs=[whole((1, ROWS, COLS)), whole((8, EXT, 128))],
        scratch_shapes=[
            pltpu.VMEM((BANDS, COLS), jnp.float32),
            pltpu.VMEM((BANDS, COLS), jnp.float32),
            pltpu.VMEM((8, ROWS, 128), jnp.float32),
        ],
    )
    return pl.pallas_call(
        wavelet_kernel,
        grid_spec=grid_spec,
        out_shape=(
            jax.ShapeDtypeStruct((1, ROWS, COLS), jnp.float32),
            jax.ShapeDtypeStruct((8, EXT, 128), jnp.float32),
        ),
        compiler_params=pltpu.CompilerParams(vmem_limit_bytes=48 * 1024 * 1024),
        name="wavelet_update",
    )(basis, field, dual_coeffs, thresholds, row_ops, column_ops)


def shifted(value, steps):
    count = lax.axis_size("strip")
    pairs = [(source, (source + steps) % count) for source in range(count)]
    return lax.ppermute(value, "strip", pairs)


def on_device(sky_image, dual_coeffs, thresholds):
    row_ops, column_ops = row_and_column_matrices()
    basis = lax.axis_index("basis").astype(jnp.int32).reshape(1)
    with jax.named_scope("rows_of_next_strip"):
        tail = shifted(sky_image[:TAIL], -1)
    with jax.named_scope("gather_columns"):
        block = jnp.concatenate([sky_image, tail], axis=0)
        field = lax.all_to_all(jnp.broadcast_to(block, (BASES, EXT, 128)), "basis", 0, 0)
    dual_next, adjoint = wavelet_update(
        basis, field, dual_coeffs, thresholds, jnp.asarray(row_ops), jnp.asarray(column_ops)
    )
    with jax.named_scope("sum_over_bases"):
        summed = jnp.sum(lax.all_to_all(adjoint, "basis", 0, 0), axis=0)
    with jax.named_scope("rows_to_next_strip"):
        carried = shifted(summed[ROWS:], 1)
        adjoint_image = summed[:ROWS] + jnp.pad(carried, ((0, ROWS - TAIL), (0, 0)))
    return (dual_next, adjoint_image)


def solution(mesh):
    placed = (P("strip", "basis"), P("basis", "strip", None), P("basis", "strip", None))
    return jax.shard_map(
        on_device,
        mesh=mesh,
        in_specs=placed,
        out_specs=(P("basis", "strip", None), P("strip", "basis")),
        check_vma=False,
    )
```

```python
import math

import jax
import jax.numpy as jnp
import ml_dtypes
import numpy as np
from jax import lax
from jax.experimental import pallas as pl
from jax.experimental.pallas import tpu as pltpu
from jax.sharding import PartitionSpec as P

BASES = 8
ROWS = 128
COLS = 1024
TILE = 256
TILES = COLS // TILE
BANDS = 224


daubechies = [
    [0.7071067811865476, 0.7071067811865476],
    [0.48296291314469025, 0.836516303737469, 0.22414386804185735, -0.12940952255092145],
    [
        0.3326705529509569,
        0.8068915093133388,
        0.4598775021193313,
        -0.13501102001039084,
        -0.08544127388224149,
        0.035226291882100656,
    ],
    [
        0.23037781330885523,
        0.7148465705525415,
        0.6308807679295904,
        -0.02798376941698385,
        -0.18703481171888114,
        0.030841381835986965,
        0.032883011666982945,
        -0.010597401784997278,
    ],
    [
        0.160102397974125,
        0.6038292697974729,
        0.7243085284385744,
        0.13842814590110342,
        -0.24229488706619015,
        -0.03224486958502952,
        0.07757149384006515,
        -0.006241490213011705,
        -0.012580751999015526,
        0.003335725285001549,
    ],
    [
        0.11154074335008017,
        0.4946238903983854,
        0.7511339080215775,
        0.3152503517092432,
        -0.22626469396516913,
        -0.12976686756709563,
        0.09750160558707936,
        0.02752286553001629,
        -0.031582039318031156,
        0.0005538422009938016,
        0.004777257511010651,
        -0.00107730108499558,
    ],
    [
        0.07785205408506236,
        0.39653931948230575,
        0.7291320908465551,
        0.4697822874053586,
        -0.14390600392910627,
        -0.22403618499416572,
        0.07130921926705004,
        0.08061260915106681,
        -0.03802993693503463,
        -0.01657454163101562,
        0.012550998556013784,
        0.00042957797300470274,
        -0.0018016407039998328,
        0.0003537138000010399,
    ],
    [
        0.05441584224308161,
        0.3128715909144659,
        0.6756307362980128,
        0.5853546836548691,
        -0.015829105256023893,
        -0.2840155429624281,
        0.00047248457399797254,
        0.128747426620186,
        -0.01736930100202211,
        -0.04408825393106472,
        0.013981027917015516,
        0.008746094047015655,
        -0.00487035299301066,
        -0.0003917403729959771,
        0.0006754494059985568,
        -0.00011747678400228192,
    ],
]


def composed_filters():
    filters = []
    for taps in daubechies:
        length = len(taps)
        low = np.zeros(16)
        high = np.zeros(16)
        low[:length] = np.float32(taps)
        high[:length] = [(-1) ** k * np.float32(taps[length - 1 - k]) for k in range(length)]
        levels = [(low, high)]
        for level in (1, 2):
            coarse = levels[-1][0]
            step = 2**level
            pair = []
            for band in (low, high):
                longer = np.zeros(len(coarse) + 15 * step)
                for k in range(16):
                    longer[k * step : k * step + len(coarse)] += band[k] * coarse
                pair.append(longer)
            levels.append(tuple(pair))
        filters.append(levels)
    return filters


def own_bands():
    odd = [(1, r) for r in range(1, ROWS, 2)]
    even = [(1, r) for r in range(0, ROWS, 2)]
    return odd + even + [(2, r) for r in range(0, ROWS, 2)] + [(3, r) for r in range(0, ROWS, 4)]


def rim_bands():
    first = [(1, r) for r in range(113, ROWS, 2)] + [(1, r) for r in range(112, ROWS, 2)]
    second = [(2, r) for start, step in ((80, 4), (82, 4), (112, 2)) for r in range(start, start + 8 * step, step)]
    third = [(3, r) for start in (16, 48, 80) for r in range(start, start + 32, 4)]
    return first + second + [None] * 8 + third + [(3, r) if r % 4 == 0 else None for r in range(112, ROWS, 2)]


def row_operator(levels, bands):
    rows = np.zeros((len(bands), 2 * ROWS))
    for at, band in enumerate(bands):
        if band is not None:
            level, row = band
            half = 2 ** (level - 1)
            taps = levels[level - 1][(row // half) % 2]
            start = row - row % (2 * half)
            rows[at, start : start + len(taps)] = taps / math.sqrt(BASES)
    return rows


def column_operators(levels):
    columns = np.zeros((3, TILE + 128, TILE))
    for level in (1, 2, 3):
        half = 2 ** (level - 1)
        for column in range(0, TILE, half):
            taps = levels[level - 1][(column // half) % 2]
            start = column - column % (2 * half)
            columns[level - 1, start : start + len(taps), column] = taps
    return columns


def two_parts(matrix):
    high = matrix.astype(ml_dtypes.bfloat16)
    low = (matrix - high.astype(np.float64)).astype(ml_dtypes.bfloat16)
    return np.stack([high, low], axis=1)


def operators():
    filters = composed_filters()
    own = np.stack([row_operator(levels, own_bands())[:, :ROWS] for levels in filters])
    rim = np.stack([row_operator(levels, rim_bands())[:, ROWS:] for levels in filters])
    columns = np.stack([column_operators(levels) for levels in filters])
    back = np.concatenate([columns[:, :, TILE:, 128:].transpose(0, 1, 3, 2), np.zeros((BASES, 3, 128, 128))], axis=3)
    columns_back = np.concatenate([back, columns[:, :, :TILE, :].transpose(0, 1, 3, 2)], axis=2)
    return [
        two_parts(m)
        for m in (np.concatenate([rim, own], axis=1), columns, columns_back, own.transpose(0, 2, 1), rim.transpose(0, 2, 1))
    ]


def split(value):
    high = value.astype(jnp.bfloat16)
    return high, (value - high.astype(jnp.float32)).astype(jnp.bfloat16)


def product(a, b):
    dot = lambda p, q: jnp.dot(p, q, preferred_element_type=jnp.float32)
    return dot(a[0], b[0]) + (dot(a[0], b[1]) + dot(a[1], b[0]))


def column_product(refs, spans, matrix_ref):
    results = []
    for level, (first, last) in enumerate(spans):
        stacked = tuple(
            jnp.concatenate([ref[first:last, t * TILE : (t + 1) * TILE + 128] for t in range(TILES)], axis=0)
            for ref in refs
        )
        out = product(stacked, (matrix_ref[0, level], matrix_ref[1, level]))
        count = last - first
        results.append([out[t * count : (t + 1) * count] for t in range(TILES)])
    return list(zip(*results))


OWN_SPANS = ((0, 128), (128, 192), (192, 224))
RIM_SPANS = ((0, 16), (16, 48), (48, 80))


def lane_masks(rows):
    column = lax.broadcasted_iota(jnp.int32, (rows, 128), 1)
    row = lax.broadcasted_iota(jnp.int32, (rows, 128), 0)
    fourth = column % 4 == 0
    return column % 2 == 0, fourth, jnp.logical_and(fourth, row % 2 == 0)


def pack(first, second, even):
    return jnp.where(even, first, pltpu.roll(second, 1, 1))


def unpack_second(packed):
    return pltpu.roll(packed, 127, 1)


def join(tiles, t):
    return jnp.concatenate([tiles[2 * t], tiles[2 * t + 1]], axis=1)


def rows_kernel(image_ref, rows_ref, columns_ref, send_ref, high_ref, low_ref, rim_high, rim_low):
    row_op = (rows_ref[0], rows_ref[1])
    for t in range(TILES):
        at = slice(t * TILE, (t + 1) * TILE)
        bands = product(row_op, split(join(image_ref, t)))
        for ref, part in zip((rim_high, rim_low, high_ref, low_ref), split(bands[:80]) + split(bands[80:])):
            ref[:, at] = part
            if t == 0:
                ref[:, COLS:] = part[:, :128]
    even, fourth, third = lane_masks(8)
    for t, (one, two, three) in enumerate(column_product((rim_high, rim_low), RIM_SPANS, columns_ref)):
        for h in range(2):
            lanes = slice(128 * h, 128 * h + 128)
            a, b, c = one[:, lanes], two[:, lanes], three[:, lanes]
            send = send_ref.at[2 * t + h]
            send[0:8] = a[0:8]
            send[8:16] = jnp.where(even, jnp.where(third, c[24:32], b[16:24]), a[8:16])
            send[16:24] = pack(jnp.where(fourth, c[16:24], b[0:8]), b[8:16], even)
            send[24:32] = pack(c[0:8], c[8:16], even)


def own_coefficients_kernel(high_ref, low_ref, columns_ref, dual_ref, base_ref):
    even, _, _ = lane_masks(64)
    _, fourth, _ = lane_masks(32)
    for t, (one, two, three) in enumerate(column_product((high_ref, low_ref), OWN_SPANS, columns_ref)):
        for h in range(2):
            lanes = slice(128 * h, 128 * h + 128)
            field = base_ref.at[2 * t + h]
            field[pl.ds(1, 64, 2), :] = one[:64, lanes]
            field[pl.ds(0, 64, 2), :] = jnp.where(even, two[:, lanes], one[64:, lanes])
            field[pl.ds(0, 32, 4), :] = jnp.where(fourth, three[:, lanes], field[pl.ds(0, 32, 4), :])
            field[...] += dual_ref[0, :, t * TILE + 128 * h : t * TILE + 128 * h + 128]


def update_kernel(base_ref, rim_ref, limit_ref, fresh_ref, send_ref):
    even, _, _ = lane_masks(8)
    for b in range(8):
        field, rim, send = fresh_ref.at[b], rim_ref.at[b], send_ref.at[b]
        field[...] = base_ref[b]
        second, third = rim[16:24], rim[24:32]
        field[pl.ds(113, 8, 2), :] += rim[0:8]
        field[pl.ds(112, 8, 2), :] += rim[8:16]
        for start, packed in ((80, second), (16, third)):
            later = start + (2 if start == 80 else 32)
            field[pl.ds(start, 8, 4), :] += jnp.where(even, packed, 0.0)
            field[pl.ds(later, 8, 4), :] += jnp.where(even, unpack_second(packed), 0.0)
        limit = limit_ref[0, :, 128 * b : 128 * b + 128]
        field[...] = jnp.minimum(jnp.maximum(field[...], -limit), limit)
        send[0:8] = field[pl.ds(113, 8, 2), :]
        send[8:16] = field[pl.ds(112, 8, 2), :]
        send[16:24] = pack(field[pl.ds(80, 8, 4), :], field[pl.ds(82, 8, 4), :], even)
        send[24:32] = pack(field[pl.ds(16, 8, 4), :], field[pl.ds(48, 8, 4), :], even)


def own_rows_kernel(fresh_ref, back_ref, rows_back_ref, next_ref, out_ref, high, low):
    even, _, third = lane_masks(64)
    for b in range(8):
        field = fresh_ref.at[b]
        next_ref[0, :, 128 * b : 128 * b + 128] = field[...]
        odd_rows, even_rows, coarse = field[pl.ds(1, 64, 2), :], field[pl.ds(0, 64, 2), :], field[pl.ds(0, 32, 4), :]
        parts = split(
            jnp.concatenate(
                [odd_rows, jnp.where(even, 0.0, even_rows), jnp.where(third, 0.0, even_rows), coarse], axis=0
            )
        )
        for ref, part in zip((high, low), parts):
            ref[:, 128 * b + 128 : 128 * b + 256] = part
            if b == 7:
                ref[:, 0:128] = part
    row_op = (rows_back_ref[0], rows_back_ref[1])
    for t, bands in enumerate(column_product((high, low), OWN_SPANS, back_ref)):
        part = product(row_op, split(jnp.concatenate(bands, axis=0)))
        out_ref[2 * t] = part[:, :128]
        out_ref[2 * t + 1] = part[:, 128:]


def rim_rows_kernel(own_ref, rim_ref, back_ref, rows_rim_ref, out_ref, high, low):
    even, fourth, third = lane_masks(8)
    for b in range(8):
        rim = rim_ref.at[b]
        odd_rows, even_rows, second, coarse = rim[0:8], rim[8:16], rim[16:24], rim[24:32]
        parts = split(
            jnp.concatenate(
                [
                    odd_rows,
                    jnp.where(even, 0.0, even_rows),
                    jnp.where(fourth, 0.0, second),
                    unpack_second(second),
                    jnp.where(third, 0.0, even_rows),
                    jnp.zeros_like(coarse),
                    coarse,
                    unpack_second(coarse),
                    second,
                    even_rows,
                ],
                axis=0,
            )
        )
        for ref, part in zip((high, low), parts):
            ref[:, 128 * b + 128 : 128 * b + 256] = part
            if b == 7:
                ref[:, 0:128] = part
    row_op = (rows_rim_ref[0], rows_rim_ref[1])
    for t, bands in enumerate(column_product((high, low), RIM_SPANS, back_ref)):
        part = product(row_op, split(jnp.concatenate(bands, axis=0)))
        out_ref[2 * t] = own_ref[2 * t] + part[:, :128]
        out_ref[2 * t + 1] = own_ref[2 * t + 1] + part[:, 128:]


F32, BF16 = jnp.float32, jnp.bfloat16
FIELD = ((BASES, ROWS, 128), F32)
RIM = ((BASES, 32, 128), F32)
WOVEN = ((1, ROWS, COLS), F32)
WIDE = ((BANDS, COLS + 128), BF16)


def call(kernel, name, out_shape, *operands, scratch=()):
    vmem = pl.BlockSpec(memory_space=pltpu.VMEM)
    return pl.pallas_call(
        kernel,
        in_specs=[vmem] * len(operands),
        out_specs=tuple(vmem for _ in out_shape),
        out_shape=tuple(jax.ShapeDtypeStruct(*o) for o in out_shape),
        scratch_shapes=[pltpu.VMEM(*s) for s in scratch],
        compiler_params=pltpu.CompilerParams(vmem_limit_bytes=32 * 1024 * 1024),
        name=name,
    )(*operands)


def shifted(value, steps):
    count = lax.axis_size("strip")
    pairs = [(source, (source + steps) % count) for source in range(count)]
    return lax.ppermute(value, "strip", pairs)


def local_update(field, dual_coeffs, thresholds, matrices, shift):
    rows, columns, columns_back, rows_back, rows_rim = matrices
    rim_scratch = ((80, COLS + 128), BF16)
    rim, high, low = call(
        rows_kernel, "row_bands", (RIM, WIDE, WIDE), field, rows, columns, scratch=(rim_scratch, rim_scratch)
    )
    with jax.named_scope("rim_coefficients"):
        rim = shift(rim, -1)
    (base,) = call(own_coefficients_kernel, "own_coefficients", (FIELD,), high, low, columns, dual_coeffs)
    fresh, rim = call(update_kernel, "clip_update", (FIELD, RIM), base, rim, thresholds)
    with jax.named_scope("rim_of_update"):
        rim = shift(rim, 1)
    dual_next, own = call(
        own_rows_kernel, "own_rows", (WOVEN, FIELD), fresh, columns_back, rows_back, scratch=(WIDE, WIDE)
    )
    (whole,) = call(
        rim_rows_kernel, "rim_rows", (FIELD,), own, rim, columns_back, rows_rim, scratch=(rim_scratch, rim_scratch)
    )
    return dual_next, whole


def on_device(sky_image, dual_coeffs, thresholds):
    basis = lax.axis_index("basis")
    matrices = [lax.dynamic_index_in_dim(jnp.asarray(m), basis, 0, False) for m in operators()]
    with jax.named_scope("gather_columns"):
        field = lax.all_to_all(jnp.broadcast_to(sky_image, (BASES, ROWS, 128)), "basis", 0, 0)
        field, *matrices = lax.optimization_barrier((field, *matrices))
    dual_next, whole = local_update(field, dual_coeffs, thresholds, matrices, shifted)
    with jax.named_scope("sum_over_bases"):
        adjoint_image = jnp.sum(lax.all_to_all(whole, "basis", 0, 0), axis=0)
    return (dual_next, adjoint_image)


def solution(mesh):
    placed = (P("strip", "basis"), P("basis", "strip", None), P("basis", "strip", None))
    return jax.shard_map(
        on_device,
        mesh=mesh,
        in_specs=placed,
        out_specs=(P("basis", "strip", None), P("strip", "basis")),
        check_vma=False,
    )
```

```python
import functools
import math

import jax
import jax.numpy as jnp
import ml_dtypes
import numpy as np
from jax import lax
from jax.experimental import pallas as pl
from jax.experimental.pallas import tpu as pltpu
from jax.sharding import PartitionSpec as P

BASES = 8
ROWS = 128
COLS = 1024
TILE = 256
TILES = COLS // TILE
BANDS = 224


daubechies = [
    [0.7071067811865476, 0.7071067811865476],
    [0.48296291314469025, 0.836516303737469, 0.22414386804185735, -0.12940952255092145],
    [
        0.3326705529509569,
        0.8068915093133388,
        0.4598775021193313,
        -0.13501102001039084,
        -0.08544127388224149,
        0.035226291882100656,
    ],
    [
        0.23037781330885523,
        0.7148465705525415,
        0.6308807679295904,
        -0.02798376941698385,
        -0.18703481171888114,
        0.030841381835986965,
        0.032883011666982945,
        -0.010597401784997278,
    ],
    [
        0.160102397974125,
        0.6038292697974729,
        0.7243085284385744,
        0.13842814590110342,
        -0.24229488706619015,
        -0.03224486958502952,
        0.07757149384006515,
        -0.006241490213011705,
        -0.012580751999015526,
        0.003335725285001549,
    ],
    [
        0.11154074335008017,
        0.4946238903983854,
        0.7511339080215775,
        0.3152503517092432,
        -0.22626469396516913,
        -0.12976686756709563,
        0.09750160558707936,
        0.02752286553001629,
        -0.031582039318031156,
        0.0005538422009938016,
        0.004777257511010651,
        -0.00107730108499558,
    ],
    [
        0.07785205408506236,
        0.39653931948230575,
        0.7291320908465551,
        0.4697822874053586,
        -0.14390600392910627,
        -0.22403618499416572,
        0.07130921926705004,
        0.08061260915106681,
        -0.03802993693503463,
        -0.01657454163101562,
        0.012550998556013784,
        0.00042957797300470274,
        -0.0018016407039998328,
        0.0003537138000010399,
    ],
    [
        0.05441584224308161,
        0.3128715909144659,
        0.6756307362980128,
        0.5853546836548691,
        -0.015829105256023893,
        -0.2840155429624281,
        0.00047248457399797254,
        0.128747426620186,
        -0.01736930100202211,
        -0.04408825393106472,
        0.013981027917015516,
        0.008746094047015655,
        -0.00487035299301066,
        -0.0003917403729959771,
        0.0006754494059985568,
        -0.00011747678400228192,
    ],
]


def composed_filters():
    filters = []
    for taps in daubechies:
        length = len(taps)
        low = np.zeros(16)
        high = np.zeros(16)
        low[:length] = np.float32(taps)
        high[:length] = [(-1) ** k * np.float32(taps[length - 1 - k]) for k in range(length)]
        levels = [(low, high)]
        for level in (1, 2):
            coarse = levels[-1][0]
            step = 2**level
            pair = []
            for band in (low, high):
                longer = np.zeros(len(coarse) + 15 * step)
                for k in range(16):
                    longer[k * step : k * step + len(coarse)] += band[k] * coarse
                pair.append(longer)
            levels.append(tuple(pair))
        filters.append(levels)
    return filters


def own_bands():
    odd = [(1, r) for r in range(1, ROWS, 2)]
    even = [(1, r) for r in range(0, ROWS, 2)]
    return odd + even + [(2, r) for r in range(0, ROWS, 2)] + [(3, r) for r in range(0, ROWS, 4)]


def rim_bands():
    first = [(1, r) for r in range(113, ROWS, 2)] + [(1, r) for r in range(112, ROWS, 2)]
    second = [(2, r) for start, step in ((80, 4), (82, 4), (112, 2)) for r in range(start, start + 8 * step, step)]
    third = [(3, r) for start in (16, 48, 80) for r in range(start, start + 32, 4)]
    return first + second + [None] * 8 + third + [(3, r) if r % 4 == 0 else None for r in range(112, ROWS, 2)]


def row_operator(levels, bands):
    rows = np.zeros((len(bands), 2 * ROWS))
    for at, band in enumerate(bands):
        if band is not None:
            level, row = band
            half = 2 ** (level - 1)
            taps = levels[level - 1][(row // half) % 2]
            start = row - row % (2 * half)
            rows[at, start : start + len(taps)] = taps / math.sqrt(BASES)
    return rows


def column_operators(levels):
    columns = np.zeros((3, 256, 128))
    for level in (1, 2, 3):
        half = 2 ** (level - 1)
        for column in range(0, 128, half):
            taps = levels[level - 1][(column // half) % 2]
            start = column - column % (2 * half)
            columns[level - 1, start : start + len(taps), column] = taps
    return columns


def two_parts(matrix):
    high = matrix.astype(ml_dtypes.bfloat16)
    return high, (matrix - high.astype(np.float64)).astype(ml_dtypes.bfloat16)


def operators():
    filters = composed_filters()
    own = np.stack([row_operator(levels, own_bands())[:, :ROWS] for levels in filters])
    rims = [row_operator(levels, rim_bands()) for levels in filters]
    before = np.stack([m[:, ROWS:] for m in rims])
    rim = np.stack([m[:, :ROWS] for m in rims])
    columns = np.stack([column_operators(levels) for levels in filters])
    columns_back = np.concatenate([columns[:, :, 128:].transpose(0, 1, 3, 2), columns[:, :, :128].transpose(0, 1, 3, 2)], axis=2)
    rows = np.concatenate([before, own, rim], axis=1)
    gap = np.zeros((BASES, ROWS, 96))
    own_back, before_back, rim_back = (m.transpose(0, 2, 1) for m in (own, before, rim))
    rows_back = np.concatenate(
        [own_back, gap[:, :, :32], before_back, before_back, gap, rim_back, rim_back], axis=2
    )
    return [
        np.stack(two_parts(np.concatenate([rows, rows], axis=2)), axis=1),
        np.concatenate(two_parts(columns), axis=3),
        np.concatenate(two_parts(columns_back), axis=3),
        np.stack(two_parts(rows_back), axis=1),
    ]


def split(value):
    high = value.astype(jnp.bfloat16)
    return high, (value - high.astype(jnp.float32)).astype(jnp.bfloat16)


def dot(a, b):
    return jnp.dot(a, b, preferred_element_type=jnp.float32)


def twice_product(rows_ref, at, field):
    stacked = jnp.concatenate([rows_ref[(0, *at)], rows_ref[(1, *at)]], axis=0)
    out = dot(stacked, jnp.concatenate(split(field), axis=0))
    count = out.shape[0] // 2
    return out[:count] + out[count:]


def column_product(refs, spans, matrix_ref):
    results = []
    for level, (first, last) in enumerate(spans):
        stacked = jnp.concatenate([ref[first:last, 128 * b : 128 * b + 256] for ref in refs for b in range(8)], axis=0)
        out = dot(stacked, matrix_ref[level])
        out = out[:, :128] + out[:, 128:]
        count = last - first
        out = out[: 8 * count] + out[8 * count :]
        results.append([out[b * count : (b + 1) * count] for b in range(8)])
    return list(zip(*results))


OWN_SPANS = ((0, 128), (128, 192), (192, 224))
RIM_SPANS = ((0, 16), (16, 48), (48, 80))


def lane_masks(rows):
    column = lax.broadcasted_iota(jnp.int32, (rows, 128), 1)
    row = lax.broadcasted_iota(jnp.int32, (rows, 128), 0)
    fourth = column % 4 == 0
    return column % 2 == 0, fourth, jnp.logical_and(fourth, row % 2 == 0)


def pack(first, second, even):
    return jnp.where(even, first, pltpu.roll(second, 1, 1))


def unpack_second(packed):
    return pltpu.roll(packed, 127, 1)


def join(tiles, t):
    return jnp.concatenate([tiles[2 * t], tiles[2 * t + 1]], axis=1)


def row_product(image_ref, rows_ref, span, high_ref, low_ref):
    for t in range(TILES):
        for ref, part in zip((high_ref, low_ref), split(twice_product(rows_ref, (span,), join(image_ref, t)))):
            ref[:, t * TILE : (t + 1) * TILE] = part
            if t == 0:
                ref[:, COLS:] = part[:, :128]


def packed_rim(field, even):
    rows = lambda start, step: field[pl.ds(start, 8, step), :]
    parts = [rows(113, 2), rows(112, 2), pack(rows(80, 4), rows(82, 4), even), pack(rows(16, 4), rows(48, 4), even)]
    return jnp.concatenate(parts, axis=0)


def rim_of_arguments_kernel(dual_ref, limit_ref, send_ref, fields):
    even, _, _ = lane_masks(8)
    for b in range(8):
        for i, ref in enumerate((dual_ref, limit_ref)):
            field = fields.at[2 * b + i]
            field[...] = ref[0, :, 128 * b : 128 * b + 128]
            send_ref[b, 32 * i : 32 * i + 32] = packed_rim(field, even)


def rim_coefficients_kernel(first, image_ref, rows_ref, columns_ref, send_ref, high, low):
    row_product(image_ref, rows_ref, slice(first, first + 80), high, low)
    even, fourth, third = lane_masks(8)
    for b, (one, two, three) in enumerate(column_product((high, low), RIM_SPANS, columns_ref)):
        send = send_ref.at[b]
        send[0:8] = one[0:8]
        send[8:16] = jnp.where(even, jnp.where(third, three[24:32], two[16:24]), one[8:16])
        send[16:24] = pack(jnp.where(fourth, three[16:24], two[0:8]), two[8:16], even)
        send[24:32] = pack(three[0:8], three[8:16], even)


def own_update_kernel(image_ref, rows_ref, columns_ref, dual_ref, limit_ref, fresh_ref, high, low):
    row_product(image_ref, rows_ref, slice(80, 304), high, low)
    even, _, _ = lane_masks(64)
    _, fourth, _ = lane_masks(32)
    for b, (one, two, three) in enumerate(column_product((high, low), OWN_SPANS, columns_ref)):
        field = fresh_ref.at[b]
        field[pl.ds(1, 64, 2), :] = one[:64]
        field[pl.ds(0, 64, 2), :] = jnp.where(even, two, one[64:])
        field[pl.ds(0, 32, 4), :] = jnp.where(fourth, three, field[pl.ds(0, 32, 4), :])
        at = slice(128 * b, 128 * b + 128)
        limit = limit_ref[0, :, at]
        field[...] = jnp.minimum(jnp.maximum(dual_ref[0, :, at] + field[...], -limit), limit)
        field[112:128] = jnp.zeros((16, 128), jnp.float32)
        for start, mask in ((80, even), (82, even), (16, fourth), (48, fourth)):
            field[pl.ds(start, 8, 4), :] = jnp.where(mask[:8], 0.0, field[pl.ds(start, 8, 4), :])


def previous_rim_kernel(image_ref, rows_ref, columns_ref, arguments_ref, out_ref, high, low, partial):
    rim_coefficients_kernel(0, image_ref, rows_ref, columns_ref, partial, high, low)
    out_ref[:, :32] = partial[...] + arguments_ref[:, :32]
    out_ref[:, 32:] = arguments_ref[:, 32:]


def rim_update_kernel(rim_ref, before_ref, send_ref):
    limit = before_ref[:, 32:]
    send_ref[...] = jnp.minimum(jnp.maximum(before_ref[:, :32] + rim_ref[...], -limit), limit)


def own_rows_kernel(fresh_ref, back_ref, rows_back_ref, out_ref, high, low):
    even, _, third = lane_masks(64)
    for b in range(8):
        field = fresh_ref.at[b]
        odd_rows, even_rows, coarse = field[pl.ds(1, 64, 2), :], field[pl.ds(0, 64, 2), :], field[pl.ds(0, 32, 4), :]
        parts = split(
            jnp.concatenate(
                [odd_rows, jnp.where(even, 0.0, even_rows), jnp.where(third, 0.0, even_rows), coarse], axis=0
            )
        )
        for ref, part in zip((high, low), parts):
            ref[:, 128 * b + 128 : 128 * b + 256] = part
            if b == 7:
                ref[:, 0:128] = part
    row_op = jnp.concatenate([rows_back_ref[0, :, :BANDS], rows_back_ref[1, :, :BANDS]], axis=0)
    tiles = [jnp.concatenate(bands, axis=0) for bands in column_product((high, low), OWN_SPANS, back_ref)]
    for t in range(TILES):
        first, second = split(join(tiles, t))
        part = dot(row_op, first)
        part = part[:ROWS] + (part[ROWS:] + dot(row_op[:ROWS], second))
        out_ref[2 * t] = part[:, :128]
        out_ref[2 * t + 1] = part[:, 128:]


def add_rim_rows(first, own_ref, rim_ref, back_ref, rows_back_ref, out_ref, high, low):
    even, fourth, third = lane_masks(8)
    for b in range(8):
        rim = rim_ref.at[b]
        odd_rows, even_rows, second, coarse = rim[0:8], rim[8:16], rim[16:24], rim[24:32]
        parts = split(
            jnp.concatenate(
                [
                    odd_rows,
                    jnp.where(even, 0.0, even_rows),
                    jnp.where(fourth, 0.0, second),
                    unpack_second(second),
                    jnp.where(third, 0.0, even_rows),
                    jnp.zeros_like(coarse),
                    coarse,
                    unpack_second(coarse),
                    second,
                    even_rows,
                ],
                axis=0,
            )
        )
        for ref, part in zip((high, low), parts):
            ref[:, 128 * b + 128 : 128 * b + 256] = part
            if b == 7:
                ref[:, 0:128] = part
    tiles = [jnp.concatenate(bands, axis=0) for bands in column_product((high, low), RIM_SPANS, back_ref)]
    for t in range(TILES):
        part = twice_product(rows_back_ref, (slice(None), slice(first, first + 160)), join(tiles, t))
        out_ref[2 * t] = own_ref[2 * t] + part[:, :128]
        out_ref[2 * t + 1] = own_ref[2 * t + 1] + part[:, 128:]


def rows_of_previous_kernel(*refs):
    add_rim_rows(256, *refs)


def finish_kernel(own_ref, rim_ref, fresh_ref, back_ref, rows_back_ref, next_ref, out_ref, high, low, fields, sent):
    even, fourth, _ = lane_masks(8)
    copies = []
    for b in range(8):
        field, rim = fields.at[b], rim_ref.at[b]
        field[...] = fresh_ref[b]
        second, third = rim[16:24], rim[24:32]
        field[pl.ds(113, 8, 2), :] = rim[0:8]
        field[pl.ds(112, 8, 2), :] = rim[8:16]
        for start, mask, value in (
            (80, even, second),
            (82, even, unpack_second(second)),
            (16, fourth, third),
            (48, fourth, unpack_second(third)),
        ):
            field[pl.ds(start, 8, 4), :] = jnp.where(mask, value, field[pl.ds(start, 8, 4), :])
        copies.append(pltpu.make_async_copy(field, next_ref.at[0, :, pl.ds(128 * b, 128)], sent.at[b]))
        copies[b].start()
    add_rim_rows(512, own_ref, rim_ref, back_ref, rows_back_ref, out_ref, high, low)
    for copy in copies:
        copy.wait()


F32, BF16 = jnp.float32, jnp.bfloat16
FIELD = ((BASES, ROWS, 128), F32)
RIM = ((BASES, 32, 128), F32)
RIMS = ((BASES, 64, 128), F32)
WOVEN = ((1, ROWS, COLS), F32)
WIDE = ((BANDS, COLS + 128), BF16)
RIM_WIDE = ((80, COLS + 128), BF16)


def call(kernel, name, out_shape, *operands, scratch=(), out_specs=None, semaphores=()):
    vmem = pl.BlockSpec(memory_space=pltpu.VMEM)
    return pl.pallas_call(
        kernel,
        in_specs=[vmem] * len(operands),
        out_specs=out_specs or tuple(vmem for _ in out_shape),
        out_shape=tuple(jax.ShapeDtypeStruct(*o) for o in out_shape),
        scratch_shapes=[pltpu.VMEM(*s) for s in scratch] + list(semaphores),
        compiler_params=pltpu.CompilerParams(vmem_limit_bytes=16 * 1024 * 1024),
        name=name,
    )(*operands)


def shifted(value, steps):
    count = lax.axis_size("strip")
    pairs = [(source, (source + steps) % count) for source in range(count)]
    return lax.ppermute(value, "strip", pairs)


def rim_of_arguments(dual_coeffs, thresholds):
    scratch = (((2 * BASES, ROWS, 128), F32),)
    (packed,) = call(
        rim_of_arguments_kernel, "rim_of_arguments", (RIMS,), dual_coeffs, thresholds, scratch=scratch
    )
    return packed


def local_update(field, arguments, dual_coeffs, thresholds, matrices, shift):
    rows, columns, columns_back, rows_back = matrices
    (rim,) = call(
        functools.partial(rim_coefficients_kernel, 304), "rim_coefficients", (RIM,), field, rows, columns,
        scratch=(RIM_WIDE, RIM_WIDE),
    )
    with jax.named_scope("rim_coefficients"):
        rim = shift(rim, 1)
    (fresh,) = call(
        own_update_kernel, "own_update", (FIELD,), field, rows, columns, dual_coeffs, thresholds, scratch=(WIDE, WIDE)
    )
    (own,) = call(own_rows_kernel, "own_rows", (FIELD,), fresh, columns_back, rows_back, scratch=(WIDE, WIDE))
    (before,) = call(
        previous_rim_kernel, "previous_rim", (RIMS,), field, rows, columns, arguments, scratch=(RIM_WIDE, RIM_WIDE, RIM)
    )
    rim, before, fresh, own = lax.optimization_barrier((rim, before, fresh, own))
    (update,) = call(rim_update_kernel, "rim_update", (RIM,), rim, before)
    with jax.named_scope("rim_of_update"):
        rim = shift(update, -1)
    (own,) = call(
        rows_of_previous_kernel, "previous_rows", (FIELD,), own, update, columns_back, rows_back, scratch=(RIM_WIDE, RIM_WIDE)
    )
    return call(
        finish_kernel,
        "finish",
        (WOVEN, FIELD),
        own, rim, fresh, columns_back, rows_back,
        scratch=(RIM_WIDE, RIM_WIDE, FIELD),
        out_specs=(pl.BlockSpec(memory_space=pl.ANY), pl.BlockSpec(memory_space=pltpu.VMEM)),
        semaphores=(pltpu.SemaphoreType.DMA((BASES,)),),
    )


def on_device(sky_image, dual_coeffs, thresholds):
    basis = lax.axis_index("basis")
    matrices = [lax.dynamic_index_in_dim(jnp.asarray(m), basis, 0, False) for m in operators()]
    with jax.named_scope("rim_of_arguments"):
        arguments = shifted(rim_of_arguments(dual_coeffs, thresholds), 1)
    with jax.named_scope("gather_columns"):
        field = lax.all_to_all(jnp.broadcast_to(sky_image, (BASES, ROWS, 128)), "basis", 0, 0)
        field, *matrices = lax.optimization_barrier((field, *matrices))
    dual_next, whole = local_update(field, arguments, dual_coeffs, thresholds, matrices, shifted)
    with jax.named_scope("sum_over_bases"):
        adjoint_image = jnp.sum(lax.all_to_all(whole, "basis", 0, 0), axis=0)
    return (dual_next, adjoint_image)


def solution(mesh):
    placed = (P("strip", "basis"), P("basis", "strip", None), P("basis", "strip", None))
    return jax.shard_map(
        on_device,
        mesh=mesh,
        in_specs=placed,
        out_specs=(P("basis", "strip", None), P("strip", "basis")),
        check_vma=False,
    )
```

```python
import functools
import math

import jax
import jax.numpy as jnp
import ml_dtypes
import numpy as np
from jax import lax
from jax.experimental import pallas as pl
from jax.experimental.pallas import tpu as pltpu
from jax.sharding import PartitionSpec as P

BASES = 8
ROWS = 128
COLS = 1024
TILE = 256
TILES = COLS // TILE
BANDS = 224


daubechies = [
    [0.7071067811865476, 0.7071067811865476],
    [0.48296291314469025, 0.836516303737469, 0.22414386804185735, -0.12940952255092145],
    [
        0.3326705529509569,
        0.8068915093133388,
        0.4598775021193313,
        -0.13501102001039084,
        -0.08544127388224149,
        0.035226291882100656,
    ],
    [
        0.23037781330885523,
        0.7148465705525415,
        0.6308807679295904,
        -0.02798376941698385,
        -0.18703481171888114,
        0.030841381835986965,
        0.032883011666982945,
        -0.010597401784997278,
    ],
    [
        0.160102397974125,
        0.6038292697974729,
        0.7243085284385744,
        0.13842814590110342,
        -0.24229488706619015,
        -0.03224486958502952,
        0.07757149384006515,
        -0.006241490213011705,
        -0.012580751999015526,
        0.003335725285001549,
    ],
    [
        0.11154074335008017,
        0.4946238903983854,
        0.7511339080215775,
        0.3152503517092432,
        -0.22626469396516913,
        -0.12976686756709563,
        0.09750160558707936,
        0.02752286553001629,
        -0.031582039318031156,
        0.0005538422009938016,
        0.004777257511010651,
        -0.00107730108499558,
    ],
    [
        0.07785205408506236,
        0.39653931948230575,
        0.7291320908465551,
        0.4697822874053586,
        -0.14390600392910627,
        -0.22403618499416572,
        0.07130921926705004,
        0.08061260915106681,
        -0.03802993693503463,
        -0.01657454163101562,
        0.012550998556013784,
        0.00042957797300470274,
        -0.0018016407039998328,
        0.0003537138000010399,
    ],
    [
        0.05441584224308161,
        0.3128715909144659,
        0.6756307362980128,
        0.5853546836548691,
        -0.015829105256023893,
        -0.2840155429624281,
        0.00047248457399797254,
        0.128747426620186,
        -0.01736930100202211,
        -0.04408825393106472,
        0.013981027917015516,
        0.008746094047015655,
        -0.00487035299301066,
        -0.0003917403729959771,
        0.0006754494059985568,
        -0.00011747678400228192,
    ],
]


def composed_filters():
    filters = []
    for taps in daubechies:
        length = len(taps)
        low = np.zeros(16)
        high = np.zeros(16)
        low[:length] = np.float32(taps)
        high[:length] = [(-1) ** k * np.float32(taps[length - 1 - k]) for k in range(length)]
        levels = [(low, high)]
        for level in (1, 2):
            coarse = levels[-1][0]
            step = 2**level
            pair = []
            for band in (low, high):
                longer = np.zeros(len(coarse) + 15 * step)
                for k in range(16):
                    longer[k * step : k * step + len(coarse)] += band[k] * coarse
                pair.append(longer)
            levels.append(tuple(pair))
        filters.append(levels)
    return filters


def own_bands():
    odd = [(1, r) for r in range(1, ROWS, 2)]
    even = [(1, r) for r in range(0, ROWS, 2)]
    return odd + even + [(2, r) for r in range(0, ROWS, 2)] + [(3, r) for r in range(0, ROWS, 4)]


def rim_bands():
    first = [(1, r) for r in range(113, ROWS, 2)] + [(1, r) for r in range(112, ROWS, 2)]
    second = [(2, r) for start, step in ((80, 4), (82, 4), (112, 2)) for r in range(start, start + 8 * step, step)]
    third = [(3, r) for start in (16, 48, 80) for r in range(start, start + 32, 4)]
    return first + second + [None] * 8 + third + [(3, r) if r % 4 == 0 else None for r in range(112, ROWS, 2)]


def row_operator(levels, bands):
    rows = np.zeros((len(bands), 2 * ROWS))
    for at, band in enumerate(bands):
        if band is not None:
            level, row = band
            half = 2 ** (level - 1)
            taps = levels[level - 1][(row // half) % 2]
            start = row - row % (2 * half)
            rows[at, start : start + len(taps)] = taps / math.sqrt(BASES)
    return rows


def column_operators(levels):
    columns = np.zeros((3, 256, 128))
    for level in (1, 2, 3):
        half = 2 ** (level - 1)
        for column in range(0, 128, half):
            taps = levels[level - 1][(column // half) % 2]
            start = column - column % (2 * half)
            columns[level - 1, start : start + len(taps), column] = taps
    return columns


def two_parts(matrix):
    high = matrix.astype(ml_dtypes.bfloat16)
    return high, (matrix - high.astype(np.float64)).astype(ml_dtypes.bfloat16)


def operators():
    filters = composed_filters()
    own = np.stack([row_operator(levels, own_bands())[:, :ROWS] for levels in filters])
    rims = [row_operator(levels, rim_bands()) for levels in filters]
    before = np.stack([m[:, ROWS:] for m in rims])
    rim = np.stack([m[:, :ROWS] for m in rims])
    columns = np.stack([column_operators(levels) for levels in filters])
    columns_back = np.concatenate([columns[:, :, 128:].transpose(0, 1, 3, 2), columns[:, :, :128].transpose(0, 1, 3, 2)], axis=2)
    levels = (slice(0, 16), slice(16, 48), slice(48, 80))
    both = np.concatenate([m[:, at] for at in levels for m in (before, rim)], axis=1)
    rows = np.concatenate([own, both], axis=1)
    rows_back = np.concatenate(
        [own.transpose(0, 2, 1), np.zeros((BASES, ROWS, 32)), both.transpose(0, 2, 1)], axis=2
    )
    return [
        np.stack(two_parts(np.concatenate([rows, rows], axis=2)), axis=1),
        np.concatenate(two_parts(columns), axis=3),
        np.concatenate(two_parts(columns_back), axis=3),
        np.stack(two_parts(rows_back), axis=1),
    ]


def split(value):
    high = value.astype(jnp.bfloat16)
    return high, (value - high.astype(jnp.float32)).astype(jnp.bfloat16)


def dot(a, b):
    return jnp.dot(a, b, preferred_element_type=jnp.float32)


def twice_product(rows_ref, at, field):
    stacked = jnp.concatenate([rows_ref[(0, *at)], rows_ref[(1, *at)]], axis=0)
    out = dot(stacked, jnp.concatenate(split(field), axis=0))
    count = out.shape[0] // 2
    return out[:count] + out[count:]


def column_product(refs, spans, matrix_ref):
    results = []
    for level, (first, last) in enumerate(spans):
        stacked = jnp.concatenate([ref[first:last, 128 * b : 128 * b + 256] for ref in refs for b in range(8)], axis=0)
        out = dot(stacked, matrix_ref[level])
        out = out[:, :128] + out[:, 128:]
        count = last - first
        out = out[: 8 * count] + out[8 * count :]
        results.append([out[b * count : (b + 1) * count] for b in range(8)])
    return list(zip(*results))


OWN_SPANS = ((0, 128), (128, 192), (192, 224))
RIM_SPANS = ((0, 32), (32, 96), (96, 160))


def lane_masks(rows):
    column = lax.broadcasted_iota(jnp.int32, (rows, 128), 1)
    row = lax.broadcasted_iota(jnp.int32, (rows, 128), 0)
    fourth = column % 4 == 0
    return column % 2 == 0, fourth, jnp.logical_and(fourth, row % 2 == 0)


def pack(first, second, even):
    return jnp.where(even, first, pltpu.roll(second, 1, 1))


def unpack_second(packed):
    return pltpu.roll(packed, 127, 1)


def join(tiles, t):
    return jnp.concatenate([tiles[2 * t], tiles[2 * t + 1]], axis=1)


def row_product(image_ref, rows_ref, span, high_ref, low_ref):
    for t in range(TILES):
        for ref, part in zip((high_ref, low_ref), split(twice_product(rows_ref, (span,), join(image_ref, t)))):
            ref[:, t * TILE : (t + 1) * TILE] = part
            if t == 0:
                ref[:, COLS:] = part[:, :128]


def packed_rim(field, even):
    rows = lambda start, step: field[pl.ds(start, 8, step), :]
    parts = [rows(113, 2), rows(112, 2), pack(rows(80, 4), rows(82, 4), even), pack(rows(16, 4), rows(48, 4), even)]
    return jnp.concatenate(parts, axis=0)


def rim_of_arguments_kernel(dual_ref, limit_ref, send_ref, fields):
    even, _, _ = lane_masks(8)
    for b in range(8):
        for i, ref in enumerate((dual_ref, limit_ref)):
            field = fields.at[2 * b + i]
            field[...] = ref[0, :, 128 * b : 128 * b + 128]
            send_ref[b, 32 * i : 32 * i + 32] = packed_rim(field, even)


def rim_coefficients_kernel(image_ref, rows_ref, columns_ref, before_ref, rim_ref, high, low):
    row_product(image_ref, rows_ref, slice(BANDS, BANDS + 160), high, low)
    even, fourth, third = lane_masks(8)
    for b, levels in enumerate(column_product((high, low), RIM_SPANS, columns_ref)):
        for i, ref in enumerate((before_ref, rim_ref)):
            one, two, three = (part[i * part.shape[0] // 2 : (i + 1) * part.shape[0] // 2] for part in levels)
            send = ref.at[b]
            send[0:8] = one[0:8]
            send[8:16] = jnp.where(even, jnp.where(third, three[24:32], two[16:24]), one[8:16])
            send[16:24] = pack(jnp.where(fourth, three[16:24], two[0:8]), two[8:16], even)
            send[24:32] = pack(three[0:8], three[8:16], even)


def own_update_kernel(image_ref, rows_ref, columns_ref, dual_ref, limit_ref, fresh_ref, high, low):
    row_product(image_ref, rows_ref, slice(0, BANDS), high, low)
    even, _, _ = lane_masks(64)
    _, fourth, _ = lane_masks(32)
    for b, (one, two, three) in enumerate(column_product((high, low), OWN_SPANS, columns_ref)):
        field = fresh_ref.at[b]
        field[pl.ds(1, 64, 2), :] = one[:64]
        field[pl.ds(0, 64, 2), :] = jnp.where(even, two, one[64:])
        field[pl.ds(0, 32, 4), :] = jnp.where(fourth, three, field[pl.ds(0, 32, 4), :])
        at = slice(128 * b, 128 * b + 128)
        limit = limit_ref[0, :, at]
        field[...] = jnp.minimum(jnp.maximum(dual_ref[0, :, at] + field[...], -limit), limit)
        field[112:128] = jnp.zeros((16, 128), jnp.float32)
        for start, mask in ((80, even), (82, even), (16, fourth), (48, fourth)):
            field[pl.ds(start, 8, 4), :] = jnp.where(mask[:8], 0.0, field[pl.ds(start, 8, 4), :])


def add_rows_back(tiles, rows_back_ref, lanes, out_ref, own_ref=None):
    row_op = jnp.concatenate([rows_back_ref[0, :, lanes], rows_back_ref[1, :, lanes]], axis=0)
    tiles = [jnp.concatenate(bands, axis=0) for bands in tiles]
    for t in range(TILES):
        first, second = split(join(tiles, t))
        part = dot(row_op, first)
        part = part[:ROWS] + (part[ROWS:] + dot(row_op[:ROWS], second))
        for h in range(2):
            half = part[:, 128 * h : 128 * h + 128]
            out_ref[2 * t + h] = half if own_ref is None else own_ref[2 * t + h] + half


def own_rows_kernel(fresh_ref, back_ref, rows_back_ref, out_ref, high, low):
    even, _, third = lane_masks(64)
    for b in range(8):
        field = fresh_ref.at[b]
        odd_rows, even_rows, coarse = field[pl.ds(1, 64, 2), :], field[pl.ds(0, 64, 2), :], field[pl.ds(0, 32, 4), :]
        parts = split(
            jnp.concatenate(
                [odd_rows, jnp.where(even, 0.0, even_rows), jnp.where(third, 0.0, even_rows), coarse], axis=0
            )
        )
        for ref, part in zip((high, low), parts):
            ref[:, 128 * b + 128 : 128 * b + 256] = part
            if b == 7:
                ref[:, 0:128] = part
    add_rows_back(column_product((high, low), OWN_SPANS, back_ref), rows_back_ref, slice(0, BANDS), out_ref)


def rim_update(first, second, arguments):
    limit = arguments[32:]
    return jnp.minimum(jnp.maximum(arguments[:32] + (first[...] + second[...]), -limit), limit)


def rim_bands_back(rim):
    even, fourth, third = lane_masks(8)
    odd_rows, even_rows, second, coarse = rim[0:8], rim[8:16], rim[16:24], rim[24:32]
    return (
        [odd_rows, jnp.where(even, 0.0, even_rows)],
        [jnp.where(fourth, 0.0, second), unpack_second(second), jnp.where(third, 0.0, even_rows), jnp.zeros_like(coarse)],
        [coarse, unpack_second(coarse), second, even_rows],
    )


def finish_kernel(
    own_ref, fresh_ref, rim_ref, ahead_ref, arguments_ref, before_ref, behind_ref, previous_ref, back_ref, rows_back_ref,
    next_ref, out_ref, high, low, fields, sent,
):
    even, fourth, _ = lane_masks(8)
    copies = []
    for b in range(8):
        field = fields.at[b]
        rim = rim_update(rim_ref.at[b], ahead_ref.at[b], arguments_ref[b])
        previous = rim_update(before_ref.at[b], behind_ref.at[b], previous_ref[b])
        field[...] = fresh_ref[b]
        second, third = rim[16:24], rim[24:32]
        field[pl.ds(113, 8, 2), :] = rim[0:8]
        field[pl.ds(112, 8, 2), :] = rim[8:16]
        for start, mask, value in (
            (80, even, second),
            (82, even, unpack_second(second)),
            (16, fourth, third),
            (48, fourth, unpack_second(third)),
        ):
            field[pl.ds(start, 8, 4), :] = jnp.where(mask, value, field[pl.ds(start, 8, 4), :])
        copies.append(pltpu.make_async_copy(field, next_ref.at[0, :, pl.ds(128 * b, 128)], sent.at[b]))
        copies[b].start()
        levels = zip(rim_bands_back(previous), rim_bands_back(rim))
        parts = split(jnp.concatenate([rows for first, second in levels for rows in first + second], axis=0))
        for ref, part in zip((high, low), parts):
            ref[:, 128 * b + 128 : 128 * b + 256] = part
            if b == 7:
                ref[:, 0:128] = part
    add_rows_back(column_product((high, low), RIM_SPANS, back_ref), rows_back_ref, slice(256, 416), out_ref, own_ref)
    for copy in copies:
        copy.wait()


F32, BF16 = jnp.float32, jnp.bfloat16
FIELD = ((BASES, ROWS, 128), F32)
RIM = ((BASES, 32, 128), F32)
RIMS = ((BASES, 64, 128), F32)
WOVEN = ((1, ROWS, COLS), F32)
WIDE = ((BANDS, COLS + 128), BF16)
RIM_WIDE = ((160, COLS + 128), BF16)


def call(kernel, name, out_shape, *operands, scratch=(), out_specs=None, semaphores=()):
    vmem = pl.BlockSpec(memory_space=pltpu.VMEM)
    return pl.pallas_call(
        kernel,
        in_specs=[vmem] * len(operands),
        out_specs=out_specs or tuple(vmem for _ in out_shape),
        out_shape=tuple(jax.ShapeDtypeStruct(*o) for o in out_shape),
        scratch_shapes=[pltpu.VMEM(*s) for s in scratch] + list(semaphores),
        compiler_params=pltpu.CompilerParams(vmem_limit_bytes=16 * 1024 * 1024),
        name=name,
    )(*operands)


def shifted(value, steps):
    count = lax.axis_size("strip")
    pairs = [(source, (source + steps) % count) for source in range(count)]
    return lax.ppermute(value, "strip", pairs)


def rim_of_arguments(dual_coeffs, thresholds):
    scratch = (((2 * BASES, ROWS, 128), F32),)
    (packed,) = call(
        rim_of_arguments_kernel, "rim_of_arguments", (RIMS,), dual_coeffs, thresholds, scratch=scratch
    )
    return packed


def local_update(field, arguments, previous, dual_coeffs, thresholds, matrices, shift):
    rows, columns, columns_back, rows_back = matrices
    before, rim = call(
        rim_coefficients_kernel, "rim_coefficients", (RIM, RIM), field, rows, columns, scratch=(RIM_WIDE, RIM_WIDE)
    )
    with jax.named_scope("rim_coefficients"):
        behind = shift(rim, 1)
        ahead = shift(before, -1)
    (fresh,) = call(
        own_update_kernel, "own_update", (FIELD,), field, rows, columns, dual_coeffs, thresholds, scratch=(WIDE, WIDE)
    )
    (own,) = call(own_rows_kernel, "own_rows", (FIELD,), fresh, columns_back, rows_back, scratch=(WIDE, WIDE))
    return call(
        finish_kernel,
        "finish",
        (WOVEN, FIELD),
        own, fresh, rim, ahead, arguments, before, behind, previous, columns_back, rows_back,
        scratch=(RIM_WIDE, RIM_WIDE, FIELD),
        out_specs=(pl.BlockSpec(memory_space=pl.ANY), pl.BlockSpec(memory_space=pltpu.VMEM)),
        semaphores=(pltpu.SemaphoreType.DMA((BASES,)),),
    )


def on_device(sky_image, dual_coeffs, thresholds):
    basis = lax.axis_index("basis")
    matrices = [lax.dynamic_index_in_dim(jnp.asarray(m), basis, 0, False) for m in operators()]
    with jax.named_scope("rim_of_arguments"):
        arguments = rim_of_arguments(dual_coeffs, thresholds)
        previous = shifted(arguments, 1)
    with jax.named_scope("gather_columns"):
        field = lax.all_to_all(jnp.broadcast_to(sky_image, (BASES, ROWS, 128)), "basis", 0, 0)
        field, *matrices = lax.optimization_barrier((field, *matrices))
    dual_next, whole = local_update(field, arguments, previous, dual_coeffs, thresholds, matrices, shifted)
    with jax.named_scope("sum_over_bases"):
        adjoint_image = jnp.sum(lax.all_to_all(whole, "basis", 0, 0), axis=0)
    return (dual_next, adjoint_image)


def solution(mesh):
    placed = (P("strip", "basis"), P("basis", "strip", None), P("basis", "strip", None))
    return jax.shard_map(
        on_device,
        mesh=mesh,
        in_specs=placed,
        out_specs=(P("basis", "strip", None), P("strip", "basis")),
        check_vma=False,
    )
```

```python
import functools
import math

import jax
import jax.numpy as jnp
import ml_dtypes
import numpy as np
from jax import lax
from jax.experimental import pallas as pl
from jax.experimental.pallas import tpu as pltpu
from jax.sharding import PartitionSpec as P

BASES = 8
ROWS = 128
COLS = 1024
TILE = 256
TILES = COLS // TILE
BANDS = 224


daubechies = [
    [0.7071067811865476, 0.7071067811865476],
    [0.48296291314469025, 0.836516303737469, 0.22414386804185735, -0.12940952255092145],
    [
        0.3326705529509569,
        0.8068915093133388,
        0.4598775021193313,
        -0.13501102001039084,
        -0.08544127388224149,
        0.035226291882100656,
    ],
    [
        0.23037781330885523,
        0.7148465705525415,
        0.6308807679295904,
        -0.02798376941698385,
        -0.18703481171888114,
        0.030841381835986965,
        0.032883011666982945,
        -0.010597401784997278,
    ],
    [
        0.160102397974125,
        0.6038292697974729,
        0.7243085284385744,
        0.13842814590110342,
        -0.24229488706619015,
        -0.03224486958502952,
        0.07757149384006515,
        -0.006241490213011705,
        -0.012580751999015526,
        0.003335725285001549,
    ],
    [
        0.11154074335008017,
        0.4946238903983854,
        0.7511339080215775,
        0.3152503517092432,
        -0.22626469396516913,
        -0.12976686756709563,
        0.09750160558707936,
        0.02752286553001629,
        -0.031582039318031156,
        0.0005538422009938016,
        0.004777257511010651,
        -0.00107730108499558,
    ],
    [
        0.07785205408506236,
        0.39653931948230575,
        0.7291320908465551,
        0.4697822874053586,
        -0.14390600392910627,
        -0.22403618499416572,
        0.07130921926705004,
        0.08061260915106681,
        -0.03802993693503463,
        -0.01657454163101562,
        0.012550998556013784,
        0.00042957797300470274,
        -0.0018016407039998328,
        0.0003537138000010399,
    ],
    [
        0.05441584224308161,
        0.3128715909144659,
        0.6756307362980128,
        0.5853546836548691,
        -0.015829105256023893,
        -0.2840155429624281,
        0.00047248457399797254,
        0.128747426620186,
        -0.01736930100202211,
        -0.04408825393106472,
        0.013981027917015516,
        0.008746094047015655,
        -0.00487035299301066,
        -0.0003917403729959771,
        0.0006754494059985568,
        -0.00011747678400228192,
    ],
]


def composed_filters():
    filters = []
    for taps in daubechies:
        length = len(taps)
        low = np.zeros(16)
        high = np.zeros(16)
        low[:length] = np.float32(taps)
        high[:length] = [(-1) ** k * np.float32(taps[length - 1 - k]) for k in range(length)]
        levels = [(low, high)]
        for level in (1, 2):
            coarse = levels[-1][0]
            step = 2**level
            pair = []
            for band in (low, high):
                longer = np.zeros(len(coarse) + 15 * step)
                for k in range(16):
                    longer[k * step : k * step + len(coarse)] += band[k] * coarse
                pair.append(longer)
            levels.append(tuple(pair))
        filters.append(levels)
    return filters


def own_bands():
    odd = [(1, r) for r in range(1, ROWS, 2)]
    even = [(1, r) for r in range(0, ROWS, 2)]
    return odd + even + [(2, r) for r in range(0, ROWS, 2)] + [(3, r) for r in range(0, ROWS, 4)]


def rim_bands():
    first = [(1, r) for r in range(113, ROWS, 2)] + [(1, r) for r in range(112, ROWS, 2)]
    second = [(2, r) for start, step in ((80, 4), (82, 4), (112, 2)) for r in range(start, start + 8 * step, step)]
    third = [(3, r) for start in (16, 48, 80) for r in range(start, start + 32, 4)]
    return first + second + [None] * 8 + third + [(3, r) if r % 4 == 0 else None for r in range(112, ROWS, 2)]


def row_operator(levels, bands):
    rows = np.zeros((len(bands), 2 * ROWS))
    for at, band in enumerate(bands):
        if band is not None:
            level, row = band
            half = 2 ** (level - 1)
            taps = levels[level - 1][(row // half) % 2]
            start = row - row % (2 * half)
            rows[at, start : start + len(taps)] = taps / math.sqrt(BASES)
    return rows


def column_operators(levels):
    columns = np.zeros((3, 256, 128))
    for level in (1, 2, 3):
        half = 2 ** (level - 1)
        for column in range(0, 128, half):
            taps = levels[level - 1][(column // half) % 2]
            start = column - column % (2 * half)
            columns[level - 1, start : start + len(taps), column] = taps
    return columns


def two_parts(matrix):
    high = matrix.astype(ml_dtypes.bfloat16)
    return high, (matrix - high.astype(np.float64)).astype(ml_dtypes.bfloat16)


def operators():
    filters = composed_filters()
    own = np.stack([row_operator(levels, own_bands())[:, :ROWS] for levels in filters])
    rims = [row_operator(levels, rim_bands()) for levels in filters]
    before = np.stack([m[:, ROWS:] for m in rims])
    rim = np.stack([m[:, :ROWS] for m in rims])
    columns = np.stack([column_operators(levels) for levels in filters])
    columns_back = np.concatenate([columns[:, :, 128:].transpose(0, 1, 3, 2), columns[:, :, :128].transpose(0, 1, 3, 2)], axis=2)
    levels = (slice(0, 16), slice(16, 48), slice(48, 80))
    both = np.concatenate([m[:, at] for at in levels for m in (before, rim)], axis=1)
    rows = np.concatenate([own, both], axis=1)
    rows_back = np.concatenate(
        [own.transpose(0, 2, 1), np.zeros((BASES, ROWS, 32)), both.transpose(0, 2, 1)], axis=2
    )
    return [
        np.stack(two_parts(np.concatenate([rows, rows], axis=2)), axis=1),
        np.concatenate(two_parts(columns), axis=3),
        np.concatenate(two_parts(columns_back), axis=3),
        np.stack(two_parts(rows_back), axis=1),
    ]


def split(value):
    high = value.astype(jnp.bfloat16)
    return high, (value - high.astype(jnp.float32)).astype(jnp.bfloat16)


def dot(a, b):
    return jnp.dot(a, b, preferred_element_type=jnp.float32)


def twice_product(rows_ref, at, field):
    stacked = jnp.concatenate([rows_ref[(0, *at)], rows_ref[(1, *at)]], axis=0)
    out = dot(stacked, jnp.concatenate(split(field), axis=0))
    count = out.shape[0] // 2
    return out[:count] + out[count:]


def column_product(refs, spans, matrix_ref):
    results = []
    for level, (first, last) in enumerate(spans):
        stacked = jnp.concatenate([ref[first:last, 128 * b : 128 * b + 256] for ref in refs for b in range(8)], axis=0)
        out = dot(stacked, matrix_ref[level])
        out = out[:, :128] + out[:, 128:]
        count = last - first
        out = out[: 8 * count] + out[8 * count :]
        results.append([out[b * count : (b + 1) * count] for b in range(8)])
    return list(zip(*results))


OWN_SPANS = ((0, 128), (128, 192), (192, 224))
RIM_SPANS = ((0, 32), (32, 96), (96, 160))


def lane_masks(rows):
    column = lax.broadcasted_iota(jnp.int32, (rows, 128), 1)
    row = lax.broadcasted_iota(jnp.int32, (rows, 128), 0)
    fourth = column % 4 == 0
    return column % 2 == 0, fourth, jnp.logical_and(fourth, row % 2 == 0)


def pack(first, second, even):
    return jnp.where(even, first, pltpu.roll(second, 1, 1))


def unpack_second(packed):
    return pltpu.roll(packed, 127, 1)


def join(tiles, t):
    return jnp.concatenate([tiles[2 * t], tiles[2 * t + 1]], axis=1)


def row_product(image_ref, rows_ref, span, high_ref, low_ref):
    for t in range(TILES):
        for ref, part in zip((high_ref, low_ref), split(twice_product(rows_ref, (span,), join(image_ref, t)))):
            ref[:, t * TILE : (t + 1) * TILE] = part
            if t == 0:
                ref[:, COLS:] = part[:, :128]


def packed_rim(field, even):
    rows = lambda start, step: field[pl.ds(start, 8, step), :]
    parts = [rows(113, 2), rows(112, 2), pack(rows(80, 4), rows(82, 4), even), pack(rows(16, 4), rows(48, 4), even)]
    return jnp.concatenate(parts, axis=0)


def rim_of_arguments_kernel(dual_ref, limit_ref, send_ref, fields):
    even, _, _ = lane_masks(8)
    for b in range(8):
        for i, ref in enumerate((dual_ref, limit_ref)):
            field = fields.at[2 * b + i]
            field[...] = ref[0, :, 128 * b : 128 * b + 128]
            send_ref[b, 32 * i : 32 * i + 32] = packed_rim(field, even)


def rim_coefficients_kernel(image_ref, rows_ref, columns_ref, before_ref, rim_ref, high, low):
    row_product(image_ref, rows_ref, slice(BANDS, BANDS + 160), high, low)
    even, fourth, third = lane_masks(8)
    for b, levels in enumerate(column_product((high, low), RIM_SPANS, columns_ref)):
        for i, ref in enumerate((before_ref, rim_ref)):
            one, two, three = (part[i * part.shape[0] // 2 : (i + 1) * part.shape[0] // 2] for part in levels)
            send = ref.at[b]
            send[0:8] = one[0:8]
            send[8:16] = jnp.where(even, jnp.where(third, three[24:32], two[16:24]), one[8:16])
            send[16:24] = pack(jnp.where(fourth, three[16:24], two[0:8]), two[8:16], even)
            send[24:32] = pack(three[0:8], three[8:16], even)


def own_update_kernel(image_ref, rows_ref, columns_ref, dual_ref, limit_ref, fresh_ref, high, low):
    row_product(image_ref, rows_ref, slice(0, BANDS), high, low)
    even, _, _ = lane_masks(64)
    _, fourth, _ = lane_masks(32)
    for b, (one, two, three) in enumerate(column_product((high, low), OWN_SPANS, columns_ref)):
        field = fresh_ref.at[b]
        field[pl.ds(1, 64, 2), :] = one[:64]
        field[pl.ds(0, 64, 2), :] = jnp.where(even, two, one[64:])
        field[pl.ds(0, 32, 4), :] = jnp.where(fourth, three, field[pl.ds(0, 32, 4), :])
        at = slice(128 * b, 128 * b + 128)
        limit = limit_ref[0, :, at]
        field[...] = jnp.minimum(jnp.maximum(dual_ref[0, :, at] + field[...], -limit), limit)
        field[112:128] = jnp.zeros((16, 128), jnp.float32)
        for start, mask in ((80, even), (82, even), (16, fourth), (48, fourth)):
            field[pl.ds(start, 8, 4), :] = jnp.where(mask[:8], 0.0, field[pl.ds(start, 8, 4), :])


def add_rows_back(tiles, rows_back_ref, lanes, out_ref, own_ref=None):
    row_op = jnp.concatenate([rows_back_ref[0, :, lanes], rows_back_ref[1, :, lanes]], axis=0)
    tiles = [jnp.concatenate(bands, axis=0) for bands in tiles]
    for t in range(TILES):
        first, second = split(join(tiles, t))
        part = dot(row_op, first)
        part = part[:ROWS] + (part[ROWS:] + dot(row_op[:ROWS], second))
        for h in range(2):
            half = part[:, 128 * h : 128 * h + 128]
            out_ref[2 * t + h] = half if own_ref is None else own_ref[2 * t + h] + half


def own_rows_kernel(fresh_ref, back_ref, rows_back_ref, out_ref, high, low):
    even, _, third = lane_masks(64)
    for b in range(8):
        field = fresh_ref.at[b]
        odd_rows, even_rows, coarse = field[pl.ds(1, 64, 2), :], field[pl.ds(0, 64, 2), :], field[pl.ds(0, 32, 4), :]
        parts = split(
            jnp.concatenate(
                [odd_rows, jnp.where(even, 0.0, even_rows), jnp.where(third, 0.0, even_rows), coarse], axis=0
            )
        )
        for ref, part in zip((high, low), parts):
            ref[:, 128 * b + 128 : 128 * b + 256] = part
            if b == 7:
                ref[:, 0:128] = part
    add_rows_back(column_product((high, low), OWN_SPANS, back_ref), rows_back_ref, slice(0, BANDS), out_ref)


def rim_update(first, second, arguments):
    limit = arguments[32:]
    return jnp.minimum(jnp.maximum(arguments[:32] + (first[...] + second[...]), -limit), limit)


def rim_bands_back(rim):
    even, fourth, third = lane_masks(8)
    odd_rows, even_rows, second, coarse = rim[0:8], rim[8:16], rim[16:24], rim[24:32]
    return (
        [odd_rows, jnp.where(even, 0.0, even_rows)],
        [jnp.where(fourth, 0.0, second), unpack_second(second), jnp.where(third, 0.0, even_rows), jnp.zeros_like(coarse)],
        [coarse, unpack_second(coarse), second, even_rows],
    )


def finish_kernel(
    own_ref, fresh_ref, rim_ref, ahead_ref, arguments_ref, before_ref, behind_ref, previous_ref, back_ref, rows_back_ref,
    next_ref, out_ref, high, low, fields, sent,
):
    even, fourth, _ = lane_masks(8)
    rims = [rim_update(rim_ref.at[b], ahead_ref.at[b], arguments_ref[b]) for b in range(8)]
    for b in range(8):
        previous = rim_update(before_ref.at[b], behind_ref.at[b], previous_ref[b])
        levels = zip(rim_bands_back(previous), rim_bands_back(rims[b]))
        parts = split(jnp.concatenate([rows for first, second in levels for rows in first + second], axis=0))
        for ref, part in zip((high, low), parts):
            ref[:, 128 * b + 128 : 128 * b + 256] = part
            if b == 7:
                ref[:, 0:128] = part
    copies = []
    for b in range(8):
        field, rim = fields.at[b], rims[b]
        field[...] = fresh_ref[b]
        second, third = rim[16:24], rim[24:32]
        field[pl.ds(113, 8, 2), :] = rim[0:8]
        field[pl.ds(112, 8, 2), :] = rim[8:16]
        for start, mask, value in (
            (80, even, second),
            (82, even, unpack_second(second)),
            (16, fourth, third),
            (48, fourth, unpack_second(third)),
        ):
            field[pl.ds(start, 8, 4), :] = jnp.where(mask, value, field[pl.ds(start, 8, 4), :])
        copies.append(pltpu.make_async_copy(field, next_ref.at[0, :, pl.ds(128 * b, 128)], sent.at[b]))
        copies[b].start()
    add_rows_back(column_product((high, low), RIM_SPANS, back_ref), rows_back_ref, slice(256, 416), out_ref, own_ref)
    for copy in copies:
        copy.wait()


F32, BF16 = jnp.float32, jnp.bfloat16
FIELD = ((BASES, ROWS, 128), F32)
RIM = ((BASES, 32, 128), F32)
RIMS = ((BASES, 64, 128), F32)
WOVEN = ((1, ROWS, COLS), F32)
WIDE = ((BANDS, COLS + 128), BF16)
RIM_WIDE = ((160, COLS + 128), BF16)


def call(kernel, name, out_shape, *operands, scratch=(), out_specs=None, semaphores=()):
    vmem = pl.BlockSpec(memory_space=pltpu.VMEM)
    return pl.pallas_call(
        kernel,
        in_specs=[vmem] * len(operands),
        out_specs=out_specs or tuple(vmem for _ in out_shape),
        out_shape=tuple(jax.ShapeDtypeStruct(*o) for o in out_shape),
        scratch_shapes=[pltpu.VMEM(*s) for s in scratch] + list(semaphores),
        compiler_params=pltpu.CompilerParams(vmem_limit_bytes=16 * 1024 * 1024),
        name=name,
    )(*operands)


def shifted(value, steps):
    count = lax.axis_size("strip")
    pairs = [(source, (source + steps) % count) for source in range(count)]
    return lax.ppermute(value, "strip", pairs)


def rim_of_arguments(dual_coeffs, thresholds):
    scratch = (((2 * BASES, ROWS, 128), F32),)
    (packed,) = call(
        rim_of_arguments_kernel, "rim_of_arguments", (RIMS,), dual_coeffs, thresholds, scratch=scratch
    )
    return packed


def local_update(field, arguments, previous, dual_coeffs, thresholds, matrices, shift):
    rows, columns, columns_back, rows_back = matrices
    before, rim = call(
        rim_coefficients_kernel, "rim_coefficients", (RIM, RIM), field, rows, columns, scratch=(RIM_WIDE, RIM_WIDE)
    )
    with jax.named_scope("rim_coefficients"):
        behind = shift(rim, 1)
        ahead = shift(before, -1)
    (fresh,) = call(
        own_update_kernel, "own_update", (FIELD,), field, rows, columns, dual_coeffs, thresholds, scratch=(WIDE, WIDE)
    )
    (own,) = call(own_rows_kernel, "own_rows", (FIELD,), fresh, columns_back, rows_back, scratch=(WIDE, WIDE))
    return call(
        finish_kernel,
        "finish",
        (WOVEN, FIELD),
        own, fresh, rim, ahead, arguments, before, behind, previous, columns_back, rows_back,
        scratch=(RIM_WIDE, RIM_WIDE, FIELD),
        out_specs=(pl.BlockSpec(memory_space=pl.ANY), pl.BlockSpec(memory_space=pltpu.VMEM)),
        semaphores=(pltpu.SemaphoreType.DMA((BASES,)),),
    )


def on_device(sky_image, dual_coeffs, thresholds):
    basis = lax.axis_index("basis")
    matrices = [lax.dynamic_index_in_dim(jnp.asarray(m), basis, 0, False) for m in operators()]
    with jax.named_scope("rim_of_arguments"):
        arguments = rim_of_arguments(dual_coeffs, thresholds)
        previous = shifted(arguments, 1)
    with jax.named_scope("gather_columns"):
        field = lax.all_to_all(jnp.broadcast_to(sky_image, (BASES, ROWS, 128)), "basis", 0, 0)
        field, *matrices = lax.optimization_barrier((field, *matrices))
    dual_next, whole = local_update(field, arguments, previous, dual_coeffs, thresholds, matrices, shifted)
    with jax.named_scope("sum_over_bases"):
        adjoint_image = jnp.sum(lax.all_to_all(whole, "basis", 0, 0), axis=0)
    return (dual_next, adjoint_image)


def solution(mesh):
    placed = (P("strip", "basis"), P("basis", "strip", None), P("basis", "strip", None))
    return jax.shard_map(
        on_device,
        mesh=mesh,
        in_specs=placed,
        out_specs=(P("basis", "strip", None), P("strip", "basis")),
        check_vma=False,
    )
```
